256 devices in a mesh: tm: 64 (over x, z, y_hi), head: 4 (over y_lo, core).
Axes of the slice: x: 4, y: 4 (y_hi: 2, y_lo: 2; y = y_hi * 2 + y_lo), z: 8, core: 2. Of those that a mesh axis runs over, the one named last changes fastest.
Arguments:
- latents: bfloat16 [49152, 3072], P('tm', 'head'), may hold values from -6 to 6
- w_query: bfloat16 [3072, 1536], P(None, 'head'), may hold values from -0.109375 to 0.109375
- w_key: bfloat16 [3072, 1536], P(None, 'head'), may hold values from -0.109375 to 0.109375
- w_value: bfloat16 [3072, 1536], P(None, 'head'), may hold values from -0.109375 to 0.109375
- q_gain: float32 [128], replicated, may hold values from 1 to 2
- k_gain: float32 [128], replicated, may hold values from 1 to 2
- w_out: bfloat16 [1536, 3072], P('head'), may hold values from -0.15625 to 0.15625
- neighbours: int32 [128, 4], P('tm'), may hold values from 0 to 127, as said below
- tile_slot: int32 [128], replicated, may hold values from 0 to 127, as said below
- slab_dest: int32 [64], replicated, may hold values from 0 to 63, as said below
Outputs:
- handed: bfloat16 [49152, 3072], P('tm', 'head')
The draws below stay inside these ranges and needn't reach their ends.
Inputs may be any that keep to these rules, and one draw needn't show every extreme that they name: `neighbours`: entry 0 of row g is g; the other 3 entries of a row are distinct tiles other than g from the slabs g // 2 - 1, g // 2 and g // 2 + 1 that exist. A permutation that keeps every tile in its own slab: tile_slot[g] // 2 == g // 2. slab_dest[s] = (s + r) % 64 for one r of 1 to 63.
All inputs are finite; a program needn't handle non-finite values.
Results may differ from the reference program's by a relative error of at most 0.012.
Values may be sent and summed in bfloat16 or wider, within the bound.
A program may use at most 128 MiB of HBM per device.

```python
import math
import jax
import jax.numpy as jnp
from jax import lax

D = 3072
HEADS = 12
HEAD_DIM = 128
TILE = 384
NB = 4
TILE_DEV = 2
TILES = 128
TOKENS = 49152
N_TM = 64
N_HEAD = 4


def draw_neighbours(key, part):
    own_tiles = jnp.arange(TILES, dtype=jnp.int32)
    slab_index = own_tiles // TILE_DEV
    offsets = jnp.arange(3 * TILE_DEV, dtype=jnp.int32)
    candidates = (slab_index[:, None] - 1) * TILE_DEV + offsets[None, :]
    usable = (candidates >= 0) & (candidates < TILES) & (candidates != own_tiles[:, None])
    noise_bits = jax.random.randint(key, (TILES, 3 * TILE_DEV), 0, 1 << 20, dtype=jnp.int32)
    ranking = jnp.where(usable, noise_bits * (3 * TILE_DEV) + offsets[None, :], -1)
    _, chosen = lax.top_k(ranking, NB - 1)
    others = jnp.take_along_axis(candidates, chosen, axis=1)
    return jnp.concatenate([own_tiles[:, None], others], axis=1).astype(jnp.int32)


def draw_tile_slot(key, part):
    slab_count = TILES // TILE_DEV
    offsets = jnp.arange(TILE_DEV, dtype=jnp.int32)
    noise_bits = jax.random.randint(key, (slab_count, TILE_DEV), 0, 1 << 20, dtype=jnp.int32) * TILE_DEV + offsets[None, :]
    ordering = jnp.argsort(noise_bits, axis=1, stable=True).astype(jnp.int32)
    placed = jnp.arange(slab_count, dtype=jnp.int32)[:, None] * TILE_DEV + ordering
    return placed.reshape(TILES).astype(jnp.int32)


def draw_slab_dest(key, part):
    slab_count = TILES // TILE_DEV
    rotation = jax.random.randint(key, (), 1, slab_count, dtype=jnp.int32)
    return ((jnp.arange(slab_count, dtype=jnp.int32) + rotation) % slab_count).astype(jnp.int32)


def block_levels(own_key, shape, split, low, top_value):
    def one(axis_at, shards_of):
        heights = jax.random.uniform(jax.random.fold_in(jax.random.fold_in(own_key, 6), axis_at), (shards_of,), jnp.float32, low / len(split), top_value / len(split))
        return jnp.repeat(jnp.exp(heights), shape[axis_at] // shards_of).reshape((-1,) + (1,) * (len(shape) - axis_at - 1))

    loudness = one(*split[0])
    for cut in split[1:]:
        loudness = loudness * one(*cut)
    return loudness


def gaussian(rng, shape, deviation, most, pieces=(), held_as=jnp.bfloat16):
    level = block_levels(rng, shape, pieces, -0.22, 0.18) if pieces else 1.0
    values = jax.random.normal(rng, shape, jnp.float32) * deviation * level
    return jnp.minimum(jnp.maximum(values, -most), most).astype(held_as)


def setup_inputs(seed: int = 0) -> dict:
    key_list = jax.random.split(jax.random.key(seed), 11)
    return {
        "latents": gaussian(key_list[0], (TOKENS, D), 1.0, 6.0, ((0, 64), (1, 4))),
        "w_query": gaussian(key_list[1], (D, HEADS * HEAD_DIM), D ** -0.5, 0.109375, ((1, 4),)),
        "w_key": gaussian(key_list[2], (D, HEADS * HEAD_DIM), D ** -0.5, 0.109375, ((1, 4),)),
        "w_value": gaussian(key_list[3], (D, HEADS * HEAD_DIM), D ** -0.5, 0.109375, ((1, 4),)),
        "q_gain": jnp.clip(jax.random.uniform(key_list[4], (HEAD_DIM,), jnp.float32, 1.0, 2.0), 1.0, 2.0),
        "k_gain": jnp.clip(jax.random.uniform(key_list[5], (HEAD_DIM,), jnp.float32, 1.0, 2.0), 1.0, 2.0),
        "w_out": gaussian(key_list[6], (HEADS * HEAD_DIM, D), (HEADS * HEAD_DIM) ** -0.5, 0.15625, ((0, 4),)),
        "neighbours": draw_neighbours(jax.random.fold_in(key_list[10], 71), 0),
        "tile_slot": draw_tile_slot(jax.random.fold_in(key_list[10], 71), 0),
        "slab_dest": draw_slab_dest(jax.random.fold_in(key_list[10], 71), 0),
    }


def normed(values_in, gain):
    mean_square = lax.optimization_barrier(jnp.mean(values_in * values_in, axis=-1, keepdims=True))
    return values_in * lax.rsqrt(mean_square + 1e-06) * gain

def reference(latents, w_query, w_key, w_value, q_gain, k_gain, w_out, neighbours, tile_slot, slab_dest):
    queries = normed(jnp.dot(latents, w_query, preferred_element_type=jnp.float32).reshape(TOKENS, HEADS, HEAD_DIM), q_gain).astype(jnp.bfloat16)
    keys_all = normed(jnp.dot(latents, w_key, preferred_element_type=jnp.float32).reshape(TOKENS, HEADS, HEAD_DIM), k_gain).astype(jnp.bfloat16)
    values_all = jnp.dot(latents, w_value, preferred_element_type=jnp.float32).astype(jnp.bfloat16).reshape(TOKENS, HEADS, HEAD_DIM)
    query_tiles = queries.reshape(TILES, TILE, HEADS, HEAD_DIM)
    key_tiles = keys_all.reshape(TILES, TILE, HEADS, HEAD_DIM)
    value_tiles = values_all.reshape(TILES, TILE, HEADS, HEAD_DIM)
    scaling = 1.0 / math.sqrt(HEAD_DIM)

    def one_tile(tile_index):
        home_block = tile_slot[tile_index]
        sources = jnp.take(tile_slot, neighbours[tile_index]).astype(jnp.int32)
        q_block = query_tiles[home_block].astype(jnp.float32)
        k_block = jnp.take(key_tiles, sources, axis=0).reshape(NB * TILE, HEADS, HEAD_DIM).astype(jnp.float32)
        v_block = jnp.take(value_tiles, sources, axis=0).reshape(NB * TILE, HEADS, HEAD_DIM).astype(jnp.float32)
        scores = jnp.einsum('qhd,khd->hqk', q_block, k_block) * scaling
        raised = jnp.exp(scores)
        probs = (raised / lax.optimization_barrier(jnp.sum(raised, axis=-1, keepdims=True))).astype(jnp.bfloat16)
        return jnp.einsum('hqk,khd->qhd', probs.astype(jnp.float32), v_block).astype(jnp.bfloat16)
    results = lax.map(one_tile, jnp.arange(TILES, dtype=jnp.int32))
    attention = jnp.zeros_like(query_tiles).at[tile_slot].set(results).reshape(TOKENS, HEADS * HEAD_DIM)
    group_width = HEADS * HEAD_DIM // N_HEAD
    total = jnp.zeros((TOKENS, D), jnp.float32)
    for group_index in range(N_HEAD):
        low = group_index * group_width
        partial_value = jnp.dot(attention[:, low:low + group_width], w_out[low:low + group_width], preferred_element_type=jnp.float32)
        partial_value = lax.optimization_barrier(partial_value.astype(jnp.bfloat16)).astype(jnp.float32)
        total = total + partial_value
    layer_out = total.astype(jnp.bfloat16)
    slabs = layer_out.reshape(N_TM, TILE_DEV * TILE, D)
    handed = jnp.zeros_like(slabs).at[slab_dest].set(slabs)
    return handed.reshape(TOKENS, D)
```

```python
import functools
import math

import jax
import jax.numpy as jnp
from jax import lax
from jax.experimental import pallas as pl
from jax.experimental.pallas import tpu as pltpu
from jax.sharding import PartitionSpec as P

HEAD_DIM = 128
MESH = pl.DeviceIdType.MESH
STEPS = 4
VMEM_LIMIT = 56 * 2**20


def other(tm):
    return tm + 1 - 2 * (tm % 2)


def core_mate(head):
    return head + 1 - 2 * (head % 2)


def across(head):
    return (head + 2) % 4


def normed(values_in, gain):
    mean_square = jnp.mean(values_in * values_in, axis=-1, keepdims=True)
    return values_in * lax.rsqrt(mean_square + 1e-06) * gain


def attend_kernel(
    lat, w_query, w_key, w_value, q_gain, k_gain, w_out, nbr, slot,
    o_ref, wo_ref,
    x, w, kv, q, send, recv, wsend, wrecv, local,
):
    tm, head = lax.axis_index("tm"), lax.axis_index("head")
    n_tm = lax.axis_size("tm")
    rows, width = lat.shape
    cols = w_query.shape[1]
    heads = cols // HEAD_DIM
    step_rows = rows // STEPS
    half = step_rows // 2
    tile = rows // 2
    pair = other(tm)
    mate, far, far_mate = core_mate(head), across(head), across(core_mate(head))
    y_hi = tm % 2
    z_to = (tm + 2 - 4 * y_hi + n_tm) % n_tm
    z_from = (tm - 2 + 4 * y_hi + n_tm) % n_tm

    loads = [
        pltpu.make_async_copy(lat, x.at[0, :, pl.ds(pl.multiple_of(head * width, width), width)], local.at[0]),
        pltpu.make_async_copy(w_query, w.at[:, pl.ds(0, cols)], local.at[1]),
        pltpu.make_async_copy(w_key, w.at[:, pl.ds(cols, cols)], local.at[2]),
        pltpu.make_async_copy(w_value, w.at[:, pl.ds(2 * cols, cols)], local.at[3]),
        pltpu.make_async_copy(
            w_out.at[:, pl.ds(pl.multiple_of(head * width, width), width)],
            wo_ref.at[pl.ds(pl.multiple_of(head * cols, cols), cols), :], local.at[4]),
    ]
    for copy in loads:
        copy.start()

    barrier = pltpu.get_barrier_semaphore()
    for device in ((tm, mate), (tm, far), (pair, far), (pair, far_mate), (z_from, head)):
        pl.semaphore_signal(barrier, inc=1, device_id=device, device_id_type=MESH)
    pl.semaphore_wait(barrier, 5)

    def band(slab, start, count, owner):
        return x.at[slab, pl.ds(start, count), pl.ds(pl.multiple_of(owner * width, width), width)]

    def copy(src, dst, kind, step, device):
        return pltpu.make_async_remote_copy(
            src_ref=src, dst_ref=dst, send_sem=send.at[kind, step], recv_sem=recv.at[kind, step],
            device_id=device, device_id_type=MESH)

    def at(step):
        return pl.multiple_of(step * step_rows, step_rows)

    def own_far(p):
        return copy(lat.at[pl.ds(at(p), step_rows), :], band(0, at(p), step_rows, head), 0, p, (tm, far))

    def own_pair(p):
        return copy(lat.at[pl.ds(at(p), step_rows), :], band(1, at(p), step_rows, head), 1, p, (pair, far))

    def relay_far(p):
        src = band(0, at(p), half, far)
        return copy(src, band(1, at(p), half, far), 2, p, (pair, far))

    def relay_pair(p):
        src = band(1, at(p) + half, half, far)
        return copy(src, band(1, at(p) + half, half, far), 3, p, (tm, far))

    def mate_own():
        return copy(lat, band(0, 0, rows, head), 4, 0, (tm, mate))

    def mate_far(p):
        block = band(0, at(p), step_rows, far)
        return copy(block, block, 5, p, (tm, mate))

    def mate_pair(p):
        block = band(1, at(p), step_rows, far)
        return copy(block, block, 6, p, (tm, mate))

    def mate_relayed(p):
        block = band(1, at(p), step_rows, head)
        return copy(block, block, 7, p, (tm, mate))

    def arrived(dst, kind, step):
        copy(dst, dst, kind, step, (tm, mate)).wait_recv()

    def kv_rows(slab, p):
        return kv.at[2 * slab + p // 2, pl.ds(pl.multiple_of((p % 2) * step_rows, step_rows), step_rows), :]

    def z_copy(p):
        return copy(kv_rows(1, p), kv_rows(2, p), 8, p, (z_to, head))

    def wo_part(owner):
        return w_out.at[:, pl.ds(pl.multiple_of(owner * width, width), width)]

    def wo_rows(owner):
        return wo_ref.at[pl.ds(pl.multiple_of(owner * cols, cols), cols), :]

    def wo_copy(k, owner, device):
        return pltpu.make_async_remote_copy(
            src_ref=wo_part(owner), dst_ref=wo_rows(head), send_sem=wsend.at[k], recv_sem=wrecv.at[k],
            device_id=device, device_id_type=MESH)

    wo_copies = [
        wo_copy(0, mate, (tm, mate)),
        wo_copy(1, far, (tm, far)),
        wo_copy(2, far_mate, (pair, far_mate)),
    ]

    for p in range(2):
        own_far(p).start()
        own_pair(p).start()
    mate_own().start()
    for copy_in in loads:
        copy_in.wait()
    arrived(band(0, 0, rows, mate), 4, 0)

    def store_kv(slab, m, key_sums, value_sums):
        b, r = 2 * slab + m // 2, pl.ds(pl.multiple_of((m % 2) * step_rows, step_rows), step_rows)
        for h in range(heads):
            c = slice(h * HEAD_DIM, (h + 1) * HEAD_DIM)
            kv[b, r, c] = normed(key_sums[:, c], k_gain[...]).astype(jnp.bfloat16)
        kv[b, r, cols:] = value_sums.astype(jnp.bfloat16)

    def step(p, carry):
        @pl.when(p < STEPS)
        def _():
            arrived(band(0, at(p), step_rows, far), 0, p)
            relay_far(p).start()
            mate_far(p).start()
            arrived(band(1, at(p), step_rows, far), 1, p)
            relay_pair(p).start()
            mate_pair(p).start()

        @pl.when(p < STEPS - 2)
        def _():
            own_far(p + 2).start()
            own_pair(p + 2).start()

        @pl.when(p == STEPS)
        def _():
            for c in wo_copies:
                c.start()

        @pl.when(p >= 1)
        def _():
            m = p - 1
            arrived(band(1, at(m), half, head), 2, m)
            arrived(band(1, at(m) + half, half, head), 3, m)
            mate_relayed(m).start()
            arrived(band(0, at(m), step_rows, far_mate), 5, m)
            arrived(band(1, at(m), step_rows, far_mate), 6, m)
            arrived(band(1, at(m), step_rows, mate), 7, m)
            sums = jnp.dot(x[1, pl.ds(at(m), step_rows), :], w[:, cols:], preferred_element_type=jnp.float32)
            store_kv(1, m, sums[:, :cols], sums[:, cols:])
            z_copy(m).start()
            sums = jnp.dot(x[0, pl.ds(at(m), step_rows), :], w[...], preferred_element_type=jnp.float32)
            for h in range(heads):
                c = slice(h * HEAD_DIM, (h + 1) * HEAD_DIM)
                q[pl.ds(at(m), step_rows), c] = normed(sums[:, c], q_gain[...]).astype(jnp.bfloat16)
            store_kv(0, m, sums[:, cols:2 * cols], sums[:, 2 * cols:])

        return carry

    lax.fori_loop(0, STEPS + 1, step, 0)

    def drain(p, carry):
        for c in (own_far(p), own_pair(p), relay_far(p), relay_pair(p), mate_far(p), mate_pair(p), mate_relayed(p)):
            c.wait_send()
        arrived(kv_rows(2, p), 8, p)
        z_copy(p).wait_send()
        return carry

    lax.fori_loop(0, STEPS, drain, 0)
    mate_own().wait_send()

    scaling = 1.0 / math.sqrt(HEAD_DIM)
    base = 2 * tm
    first = slot[base] - base

    def attend(b, carry):
        t = jnp.clip(first + b - 2 * first * b, 0, 1)
        places = []
        for j in range(nbr.shape[1]):
            block = slot[jnp.clip(nbr[t, j], 0, slot.shape[0] - 1)] - base
            block = jnp.where(block < 0, block + 6 - 2 * y_hi, jnp.where(block >= 2, block + 2 * y_hi, block))
            places.append(jnp.clip(block, 0, kv.shape[0] - 1))
        r = pl.ds(pl.multiple_of(b * tile, tile), tile)
        for h in range(heads):
            c = slice(h * HEAD_DIM, (h + 1) * HEAD_DIM)
            cv = slice(cols + h * HEAD_DIM, cols + (h + 1) * HEAD_DIM)
            qh = q[r, c]
            total, out = None, None
            for place in places:
                scores = lax.dot_general(
                    qh, kv[place, :, c], (((1,), (1,)), ((), ())), preferred_element_type=jnp.float32)
                raised = jnp.exp(scores * scaling)
                part = jnp.sum(raised, axis=-1, keepdims=True)
                got = jnp.dot(raised.astype(jnp.bfloat16), kv[place, :, cv], preferred_element_type=jnp.float32)
                total = part if total is None else total + part
                out = got if out is None else out + got
            o_ref[r, c] = (out / total).astype(jnp.bfloat16)
        return carry

    lax.fori_loop(0, 2, attend, 0)

    for k, owner in enumerate((mate, far, far_mate)):
        wo_copies[k].wait_send()
        pltpu.make_async_remote_copy(
            src_ref=wo_rows(owner), dst_ref=wo_rows(owner), send_sem=wsend.at[k], recv_sem=wrecv.at[k],
            device_id=(tm, mate), device_id_type=MESH).wait_recv()


def output_kernel(o, wo, out, g, send, recv, local):
    tm, head = lax.axis_index("tm"), lax.axis_index("head")
    rows, cols = o.shape
    step_rows = rows // STEPS
    mate, far, far_mate = core_mate(head), across(head), across(core_mate(head))

    def band(start, count, owner):
        return g.at[pl.ds(start, count), pl.ds(pl.multiple_of(owner * cols, cols), cols)]

    def at(step):
        return pl.multiple_of(step * step_rows, step_rows)

    own = pltpu.make_async_copy(o, band(0, rows, head), local)
    own.start()
    barrier = pltpu.get_barrier_semaphore()
    for device in ((tm, mate), (tm, far)):
        pl.semaphore_signal(barrier, inc=1, device_id=device, device_id_type=MESH)
    pl.semaphore_wait(barrier, 2)

    def copy(src, dst, kind, step, device):
        return pltpu.make_async_remote_copy(
            src_ref=src, dst_ref=dst, send_sem=send.at[kind, step], recv_sem=recv.at[kind, step],
            device_id=device, device_id_type=MESH)

    def own_far(p):
        return copy(o.at[pl.ds(at(p), step_rows), :], band(at(p), step_rows, head), 0, p, (tm, far))

    def own_mate(p):
        return copy(o.at[pl.ds(at(p), step_rows), :], band(at(p), step_rows, head), 1, p, (tm, mate))

    def far_to_mate(p):
        block = band(at(p), step_rows, far)
        return copy(block, block, 2, p, (tm, mate))

    def arrived(dst, kind, step):
        copy(dst, dst, kind, step, (tm, mate)).wait_recv()

    for p in range(STEPS):
        own_far(p).start()
        own_mate(p).start()
    own.wait()

    def step(p, carry):
        arrived(band(at(p), step_rows, far), 0, p)
        far_to_mate(p).start()
        arrived(band(at(p), step_rows, mate), 1, p)
        arrived(band(at(p), step_rows, far_mate), 2, p)
        r = pl.ds(at(p), step_rows)
        out[r, :] = jnp.dot(g[r, :], wo[...], preferred_element_type=jnp.float32).astype(jnp.bfloat16)
        return carry

    lax.fori_loop(0, STEPS, step, 0)

    def drain(p, carry):
        for c in (own_far(p), own_mate(p), far_to_mate(p)):
            c.wait_send()
        return carry

    lax.fori_loop(0, STEPS, drain, 0)


def per_device(
    latents, w_query, w_key, w_value, q_gain, k_gain, w_out, neighbours, tile_slot, slab_dest
):
    rows, width = latents.shape
    cols = w_query.shape[1]
    any_spec = pl.BlockSpec(memory_space=pl.ANY)
    vmem_spec = pl.BlockSpec(memory_space=pltpu.VMEM)
    smem_spec = pl.BlockSpec(memory_space=pltpu.SMEM)
    bf16 = jnp.bfloat16
    attention, wo = pl.pallas_call(
        attend_kernel,
        name="attend",
        out_shape=(
            jax.ShapeDtypeStruct((rows, cols), bf16),
            jax.ShapeDtypeStruct((4 * cols, width), bf16),
        ),
        in_specs=[any_spec] * 4 + [vmem_spec] * 2 + [any_spec] + [smem_spec] * 2,
        out_specs=(vmem_spec, vmem_spec),
        scratch_shapes=[
            pltpu.VMEM((2, rows, 4 * width), bf16),
            pltpu.VMEM((4 * width, 3 * cols), bf16),
            pltpu.VMEM((6, rows // 2, 2 * cols), bf16),
            pltpu.VMEM((rows, cols), bf16),
            pltpu.SemaphoreType.DMA((9, STEPS)),
            pltpu.SemaphoreType.DMA((9, STEPS)),
            pltpu.SemaphoreType.DMA((3,)),
            pltpu.SemaphoreType.DMA((3,)),
            pltpu.SemaphoreType.DMA((5,)),
        ],
        compiler_params=pltpu.CompilerParams(
            collective_id=1, has_side_effects=True, vmem_limit_bytes=VMEM_LIMIT
        ),
    )(
        latents, w_query, w_key, w_value, q_gain.reshape(1, -1), k_gain.reshape(1, -1), w_out, neighbours, tile_slot
    )
    n_tm = lax.axis_size("tm")
    moves = [
        functools.partial(lax.ppermute, axis_name="tm", perm=[(i, (i + r) % n_tm) for i in range(n_tm)])
        for r in range(1, n_tm)
    ]
    attention = lax.switch(slab_dest[0] - 1, moves, attention)
    return pl.pallas_call(
        output_kernel,
        name="output",
        out_shape=jax.ShapeDtypeStruct((rows, width), bf16),
        in_specs=[any_spec, vmem_spec],
        out_specs=vmem_spec,
        scratch_shapes=[
            pltpu.VMEM((rows, 4 * cols), bf16),
            pltpu.SemaphoreType.DMA((3, STEPS)),
            pltpu.SemaphoreType.DMA((3, STEPS)),
            pltpu.SemaphoreType.DMA,
        ],
        compiler_params=pltpu.CompilerParams(
            collective_id=2, has_side_effects=True, vmem_limit_bytes=VMEM_LIMIT
        ),
    )(attention, wo)


def solution(mesh):
    return jax.shard_map(
        per_device,
        mesh=mesh,
        in_specs=(
            P("tm", "head"),
            P(None, "head"),
            P(None, "head"),
            P(None, "head"),
            P(),
            P(),
            P("head", None),
            P("tm", None),
            P(),
            P(),
        ),
        out_specs=P("tm", "head"),
        check_vma=False,
    )
```

```python
import functools
import math

import jax
import jax.numpy as jnp
from jax import lax
from jax.experimental import pallas as pl
from jax.experimental.pallas import tpu as pltpu
from jax.sharding import PartitionSpec as P

HEAD_DIM = 128
MESH = pl.DeviceIdType.MESH
STEPS = 4
VMEM_LIMIT = 56 * 2**20


def other(tm):
    return tm + 1 - 2 * (tm % 2)


def core_mate(head):
    return head + 1 - 2 * (head % 2)


def across(head):
    return (head + 2) % 4


def normed(values_in, gain):
    mean_square = jnp.mean(values_in * values_in, axis=-1, keepdims=True)
    return values_in * lax.rsqrt(mean_square + 1e-06) * gain


def attend_kernel(
    lat, w_query, w_key, w_value, q_gain, k_gain, w_out, nbr, slot,
    o_ref, wo_ref,
    x, w, kv, q, send, recv, wsend, wrecv, local,
):
    tm, head = lax.axis_index("tm"), lax.axis_index("head")
    n_tm = lax.axis_size("tm")
    rows, width = lat.shape
    cols = w_query.shape[1]
    heads = cols // HEAD_DIM
    step_rows = rows // STEPS
    half = step_rows // 2
    tile = rows // 2
    pair = other(tm)
    mate, far, far_mate = core_mate(head), across(head), across(core_mate(head))
    y_hi = tm % 2
    z_to = (tm + 2 - 4 * y_hi + n_tm) % n_tm
    z_from = (tm - 2 + 4 * y_hi + n_tm) % n_tm

    loads = [
        pltpu.make_async_copy(lat, x.at[0, :, pl.ds(pl.multiple_of(head * width, width), width)], local.at[0]),
        pltpu.make_async_copy(w_query, w.at[:, pl.ds(0, cols)], local.at[1]),
        pltpu.make_async_copy(w_key, w.at[:, pl.ds(cols, cols)], local.at[2]),
        pltpu.make_async_copy(w_value, w.at[:, pl.ds(2 * cols, cols)], local.at[3]),
        pltpu.make_async_copy(
            w_out.at[:, pl.ds(pl.multiple_of(head * width, width), width)],
            wo_ref.at[pl.ds(pl.multiple_of(head * cols, cols), cols), :], local.at[4]),
    ]
    for copy in loads:
        copy.start()

    barrier = pltpu.get_barrier_semaphore()
    for device in ((tm, mate), (tm, far), (pair, far), (pair, far_mate), (z_from, head)):
        pl.semaphore_signal(barrier, inc=1, device_id=device, device_id_type=MESH)
    pl.semaphore_wait(barrier, 5)

    def band(slab, start, count, owner):
        return x.at[slab, pl.ds(start, count), pl.ds(pl.multiple_of(owner * width, width), width)]

    def copy(src, dst, kind, step, device):
        return pltpu.make_async_remote_copy(
            src_ref=src, dst_ref=dst, send_sem=send.at[kind, step], recv_sem=recv.at[kind, step],
            device_id=device, device_id_type=MESH)

    def at(step):
        return pl.multiple_of(step * step_rows, step_rows)

    def own_far(p):
        return copy(lat.at[pl.ds(at(p), step_rows), :], band(0, at(p), step_rows, head), 0, p, (tm, far))

    def own_pair(p):
        return copy(lat.at[pl.ds(at(p), step_rows), :], band(1, at(p), step_rows, head), 1, p, (pair, far))

    def relay_far(p):
        src = band(0, at(p), half, far)
        return copy(src, band(1, at(p), half, far), 2, p, (pair, far))

    def relay_pair(p):
        src = band(1, at(p) + half, half, far)
        return copy(src, band(1, at(p) + half, half, far), 3, p, (tm, far))

    def mate_own():
        return copy(lat, band(0, 0, rows, head), 4, 0, (tm, mate))

    def mate_far(p):
        block = band(0, at(p), step_rows, far)
        return copy(block, block, 5, p, (tm, mate))

    def mate_pair(p):
        block = band(1, at(p), step_rows, far)
        return copy(block, block, 6, p, (tm, mate))

    def mate_relayed(p):
        block = band(1, at(p), step_rows, head)
        return copy(block, block, 7, p, (tm, mate))

    def arrived(dst, kind, step):
        copy(dst, dst, kind, step, (tm, mate)).wait_recv()

    def kv_rows(slab, p):
        return kv.at[2 * slab + p // 2, pl.ds(pl.multiple_of((p % 2) * step_rows, step_rows), step_rows), :]

    def z_copy(p):
        return copy(kv_rows(1, p), kv_rows(2, p), 8, p, (z_to, head))

    def wo_part(owner):
        return w_out.at[:, pl.ds(pl.multiple_of(owner * width, width), width)]

    def wo_rows(owner):
        return wo_ref.at[pl.ds(pl.multiple_of(owner * cols, cols), cols), :]

    def wo_copy(k, owner, device):
        return pltpu.make_async_remote_copy(
            src_ref=wo_part(owner), dst_ref=wo_rows(head), send_sem=wsend.at[k], recv_sem=wrecv.at[k],
            device_id=device, device_id_type=MESH)

    wo_copies = [
        wo_copy(0, mate, (tm, mate)),
        wo_copy(1, far, (tm, far)),
        wo_copy(2, far_mate, (pair, far_mate)),
    ]

    for p in range(2):
        own_far(p).start()
        own_pair(p).start()
    mate_own().start()
    for copy_in in loads:
        copy_in.wait()
    arrived(band(0, 0, rows, mate), 4, 0)

    def store_kv(slab, m, key_sums, value_sums):
        b, r = 2 * slab + m // 2, pl.ds(pl.multiple_of((m % 2) * step_rows, step_rows), step_rows)
        for h in range(heads):
            c = slice(h * HEAD_DIM, (h + 1) * HEAD_DIM)
            kv[b, r, c] = normed(key_sums[:, c], k_gain[...]).astype(jnp.bfloat16)
        kv[b, r, cols:] = value_sums.astype(jnp.bfloat16)

    def step(p, carry):
        @pl.when(p < STEPS)
        def _():
            arrived(band(0, at(p), step_rows, far), 0, p)
            relay_far(p).start()
            mate_far(p).start()
            arrived(band(1, at(p), step_rows, far), 1, p)
            relay_pair(p).start()
            mate_pair(p).start()

        @pl.when(p < STEPS - 2)
        def _():
            own_far(p + 2).start()
            own_pair(p + 2).start()

        @pl.when(p == STEPS)
        def _():
            for c in wo_copies:
                c.start()

        @pl.when(p >= 1)
        def _():
            m = p - 1
            arrived(band(1, at(m), half, head), 2, m)
            arrived(band(1, at(m) + half, half, head), 3, m)
            mate_relayed(m).start()
            arrived(band(0, at(m), step_rows, far_mate), 5, m)
            arrived(band(1, at(m), step_rows, far_mate), 6, m)
            arrived(band(1, at(m), step_rows, mate), 7, m)
            sums = jnp.dot(x[1, pl.ds(at(m), step_rows), :], w[:, cols:], preferred_element_type=jnp.float32)
            store_kv(1, m, sums[:, :cols], sums[:, cols:])
            z_copy(m).start()
            sums = jnp.dot(x[0, pl.ds(at(m), step_rows), :], w[...], preferred_element_type=jnp.float32)
            for h in range(heads):
                c = slice(h * HEAD_DIM, (h + 1) * HEAD_DIM)
                q[pl.ds(at(m), step_rows), c] = normed(sums[:, c], q_gain[...]).astype(jnp.bfloat16)
            store_kv(0, m, sums[:, cols:2 * cols], sums[:, 2 * cols:])

        return carry

    lax.fori_loop(0, STEPS + 1, step, 0)

    def drain(p, carry):
        for c in (own_far(p), own_pair(p), relay_far(p), relay_pair(p), mate_far(p), mate_pair(p), mate_relayed(p)):
            c.wait_send()
        arrived(kv_rows(2, p), 8, p)
        z_copy(p).wait_send()
        return carry

    lax.fori_loop(0, STEPS, drain, 0)
    mate_own().wait_send()

    scaling = 1.0 / math.sqrt(HEAD_DIM)
    base = 2 * tm
    first = slot[base] - base

    def attend(b, carry):
        t = jnp.clip(first + b - 2 * first * b, 0, 1)
        places = []
        for j in range(nbr.shape[1]):
            block = slot[jnp.clip(nbr[t, j], 0, slot.shape[0] - 1)] - base
            block = jnp.where(block < 0, block + 6 - 2 * y_hi, jnp.where(block >= 2, block + 2 * y_hi, block))
            places.append(jnp.clip(block, 0, kv.shape[0] - 1))
        r = pl.ds(pl.multiple_of(b * tile, tile), tile)
        for h in range(heads):
            c = slice(h * HEAD_DIM, (h + 1) * HEAD_DIM)
            cv = slice(cols + h * HEAD_DIM, cols + (h + 1) * HEAD_DIM)
            qh = q[r, c]
            total, out = None, None
            for place in places:
                scores = lax.dot_general(
                    qh, kv[place, :, c], (((1,), (1,)), ((), ())), preferred_element_type=jnp.float32)
                raised = jnp.exp(scores * scaling)
                part = jnp.sum(raised, axis=-1, keepdims=True)
                got = jnp.dot(raised.astype(jnp.bfloat16), kv[place, :, cv], preferred_element_type=jnp.float32)
                total = part if total is None else total + part
                out = got if out is None else out + got
            o_ref[r, c] = (out / total).astype(jnp.bfloat16)
        return carry

    lax.fori_loop(0, 2, attend, 0)

    for k, owner in enumerate((mate, far, far_mate)):
        wo_copies[k].wait_send()
        pltpu.make_async_remote_copy(
            src_ref=wo_rows(owner), dst_ref=wo_rows(owner), send_sem=wsend.at[k], recv_sem=wrecv.at[k],
            device_id=(tm, mate), device_id_type=MESH).wait_recv()


def hand_kernel(r, o, g, send, recv):
    tm, head = lax.axis_index("tm"), lax.axis_index("head")
    n_tm = lax.axis_size("tm")
    rows, cols = o.shape
    mate, far, far_mate = core_mate(head), across(head), across(core_mate(head))
    to, source = (tm + r) % n_tm, (tm - r + n_tm) % n_tm
    step_rows = rows // STEPS

    def band(start, count, owner):
        return g.at[pl.ds(start, count), pl.ds(pl.multiple_of(owner * cols, cols), cols)]

    def at(step):
        return pl.multiple_of(step * step_rows, step_rows)

    barrier = pltpu.get_barrier_semaphore()
    for device in ((tm, mate), (tm, far), (source, head)):
        pl.semaphore_signal(barrier, inc=1, device_id=device, device_id_type=MESH)
    pl.semaphore_wait(barrier, 3)

    def copy(src, dst, kind, step, device):
        return pltpu.make_async_remote_copy(
            src_ref=src, dst_ref=dst, send_sem=send.at[kind, step], recv_sem=recv.at[kind, step],
            device_id=device, device_id_type=MESH)

    def hand(p):
        return copy(o.at[pl.ds(at(p), step_rows), :], band(at(p), step_rows, head), 0, p, (to, head))

    def pass_on(p, owner, kind, device):
        block = band(at(p), step_rows, owner)
        return copy(block, block, kind, p, device)

    def start(p, carry):
        hand(p).start()
        return carry

    def first(p, carry):
        pass_on(p, head, 0, (tm, mate)).wait_recv()
        pass_on(p, head, 1, (tm, far)).start()
        pass_on(p, head, 2, (tm, mate)).start()
        return carry

    def second(p, carry):
        pass_on(p, far, 1, (tm, mate)).wait_recv()
        pass_on(p, far, 3, (tm, mate)).start()
        return carry

    def last(p, carry):
        pass_on(p, mate, 2, (tm, mate)).wait_recv()
        pass_on(p, far_mate, 3, (tm, mate)).wait_recv()
        hand(p).wait_send()
        pass_on(p, head, 1, (tm, far)).wait_send()
        pass_on(p, head, 2, (tm, mate)).wait_send()
        pass_on(p, far, 3, (tm, mate)).wait_send()
        return carry

    for body in (start, first, second, last):
        lax.fori_loop(0, STEPS, body, 0)


def handed_over(r, o):
    rows, cols = o.shape
    return pl.pallas_call(
        functools.partial(hand_kernel, r),
        name="hand",
        out_shape=jax.ShapeDtypeStruct((rows, 4 * cols), jnp.bfloat16),
        in_specs=[pl.BlockSpec(memory_space=pl.ANY)],
        out_specs=pl.BlockSpec(memory_space=pl.ANY),
        scratch_shapes=[
            pltpu.SemaphoreType.DMA((4, STEPS)),
            pltpu.SemaphoreType.DMA((4, STEPS)),
        ],
        compiler_params=pltpu.CompilerParams(
            collective_id=2 + r, has_side_effects=True, vmem_limit_bytes=VMEM_LIMIT
        ),
    )(o)


def product_kernel(g, wo, out):
    step_rows = 256
    def step(p, carry):
        r = pl.ds(pl.multiple_of(p * step_rows, step_rows), step_rows)
        out[r, :] = jnp.dot(g[r, :], wo[...], preferred_element_type=jnp.float32).astype(jnp.bfloat16)
        return carry
    lax.fori_loop(0, out.shape[0] // step_rows, step, 0)


def per_device(
    latents, w_query, w_key, w_value, q_gain, k_gain, w_out, neighbours, tile_slot, slab_dest
):
    rows, width = latents.shape
    cols = w_query.shape[1]
    any_spec = pl.BlockSpec(memory_space=pl.ANY)
    vmem_spec = pl.BlockSpec(memory_space=pltpu.VMEM)
    smem_spec = pl.BlockSpec(memory_space=pltpu.SMEM)
    bf16 = jnp.bfloat16
    attention, wo = pl.pallas_call(
        attend_kernel,
        name="attend",
        out_shape=(
            jax.ShapeDtypeStruct((rows, cols), bf16),
            jax.ShapeDtypeStruct((4 * cols, width), bf16),
        ),
        in_specs=[any_spec] * 4 + [vmem_spec] * 2 + [any_spec] + [smem_spec] * 2,
        out_specs=(vmem_spec, vmem_spec),
        scratch_shapes=[
            pltpu.VMEM((2, rows, 4 * width), bf16),
            pltpu.VMEM((4 * width, 3 * cols), bf16),
            pltpu.VMEM((6, rows // 2, 2 * cols), bf16),
            pltpu.VMEM((rows, cols), bf16),
            pltpu.SemaphoreType.DMA((9, STEPS)),
            pltpu.SemaphoreType.DMA((9, STEPS)),
            pltpu.SemaphoreType.DMA((3,)),
            pltpu.SemaphoreType.DMA((3,)),
            pltpu.SemaphoreType.DMA((5,)),
        ],
        compiler_params=pltpu.CompilerParams(
            collective_id=1, has_side_effects=True, vmem_limit_bytes=VMEM_LIMIT
        ),
    )(
        latents, w_query, w_key, w_value, q_gain.reshape(1, -1), k_gain.reshape(1, -1), w_out, neighbours, tile_slot
    )
    n_tm = lax.axis_size("tm")
    hands = [functools.partial(handed_over, r) for r in range(1, n_tm)]
    gathered = lax.switch(slab_dest[0] - 1, hands, attention)
    return pl.pallas_call(
        product_kernel,
        name="product",
        out_shape=jax.ShapeDtypeStruct((rows, width), bf16),
        in_specs=[vmem_spec, vmem_spec],
        out_specs=vmem_spec,
        compiler_params=pltpu.CompilerParams(vmem_limit_bytes=VMEM_LIMIT),
    )(gathered, wo)


def solution(mesh):
    return jax.shard_map(
        per_device,
        mesh=mesh,
        in_specs=(
            P("tm", "head"),
            P(None, "head"),
            P(None, "head"),
            P(None, "head"),
            P(),
            P(),
            P("head", None),
            P("tm", None),
            P(),
            P(),
        ),
        out_specs=P("tm", "head"),
        check_vma=False,
    )
```

```python
import functools
import math

import jax
import jax.numpy as jnp
from jax import lax
from jax.experimental import pallas as pl
from jax.experimental.pallas import tpu as pltpu
from jax.sharding import PartitionSpec as P

HEAD_DIM = 128
MESH = pl.DeviceIdType.MESH
STEPS = 4
SAME_X = 16
N_Z = 8
CHUNKS = 8
HAND_LIMIT = 4 * 2**20
PRODUCT_LIMIT = 16 * 2**20
VMEM_LIMIT = 56 * 2**20


def other(tm):
    return tm + 1 - 2 * (tm % 2)


def core_mate(head):
    return head + 1 - 2 * (head % 2)


def across(head):
    return (head + 2) % 4


def normed(values_in, gain):
    mean_square = jnp.mean(values_in * values_in, axis=-1, keepdims=True)
    return values_in * lax.rsqrt(mean_square + 1e-06) * gain


def attend_kernel(
    lat, w_query, w_key, w_value, q_gain, k_gain, w_out, nbr, slot,
    o_ref, wo_ref,
    x, w, kv, q, send, recv, wsend, wrecv, local,
):
    tm, head = lax.axis_index("tm"), lax.axis_index("head")
    n_tm = lax.axis_size("tm")
    rows, width = lat.shape
    cols = w_query.shape[1]
    heads = cols // HEAD_DIM
    step_rows = rows // STEPS
    half = step_rows // 2
    tile = rows // 2
    pair = other(tm)
    mate, far, far_mate = core_mate(head), across(head), across(core_mate(head))
    y_hi = tm % 2
    z_to = (tm + 2 - 4 * y_hi + n_tm) % n_tm
    z_from = (tm - 2 + 4 * y_hi + n_tm) % n_tm

    loads = [
        pltpu.make_async_copy(lat, x.at[0, :, pl.ds(pl.multiple_of(head * width, width), width)], local.at[0]),
        pltpu.make_async_copy(w_query, w.at[:, pl.ds(0, cols)], local.at[1]),
        pltpu.make_async_copy(w_key, w.at[:, pl.ds(cols, cols)], local.at[2]),
        pltpu.make_async_copy(w_value, w.at[:, pl.ds(2 * cols, cols)], local.at[3]),
        pltpu.make_async_copy(
            w_out.at[:, pl.ds(pl.multiple_of(head * width, width), width)],
            wo_ref.at[pl.ds(pl.multiple_of(head * cols, cols), cols), :], local.at[4]),
    ]
    barrier = pltpu.get_barrier_semaphore()
    for device in ((tm, mate), (tm, far), (pair, far), (pair, far_mate), (z_from, head)):
        pl.semaphore_signal(barrier, inc=1, device_id=device, device_id_type=MESH)
    pl.semaphore_wait(barrier, 5)

    def band(slab, start, count, owner):
        return x.at[slab, pl.ds(start, count), pl.ds(pl.multiple_of(owner * width, width), width)]

    def copy(src, dst, kind, step, device):
        return pltpu.make_async_remote_copy(
            src_ref=src, dst_ref=dst, send_sem=send.at[kind, step], recv_sem=recv.at[kind, step],
            device_id=device, device_id_type=MESH)

    def at(step):
        return pl.multiple_of(step * step_rows, step_rows)

    def own_far(p):
        return copy(lat.at[pl.ds(at(p), step_rows), :], band(0, at(p), step_rows, head), 0, p, (tm, far))

    def own_pair(p):
        return copy(lat.at[pl.ds(at(p), step_rows), :], band(1, at(p), step_rows, head), 1, p, (pair, far))

    def relay_far(p):
        src = band(0, at(p), half, far)
        return copy(src, band(1, at(p), half, far), 2, p, (pair, far))

    def relay_pair(p):
        src = band(1, at(p) + half, half, far)
        return copy(src, band(1, at(p) + half, half, far), 3, p, (tm, far))

    def mate_own():
        return copy(lat, band(0, 0, rows, head), 4, 0, (tm, mate))

    def mate_far(p):
        block = band(0, at(p), step_rows, far)
        return copy(block, block, 5, p, (tm, mate))

    def mate_pair(p):
        block = band(1, at(p), step_rows, far)
        return copy(block, block, 6, p, (tm, mate))

    def mate_relayed(p):
        block = band(1, at(p), step_rows, head)
        return copy(block, block, 7, p, (tm, mate))

    def arrived(dst, kind, step):
        copy(dst, dst, kind, step, (tm, mate)).wait_recv()

    def kv_rows(slab, p):
        return kv.at[2 * slab + p // 2, pl.ds(pl.multiple_of((p % 2) * step_rows, step_rows), step_rows), :]

    def z_copy(p):
        return copy(kv_rows(1, p), kv_rows(2, p), 8, p, (z_to, head))

    def wo_part(owner):
        return w_out.at[:, pl.ds(pl.multiple_of(owner * width, width), width)]

    def wo_rows(owner):
        return wo_ref.at[pl.ds(pl.multiple_of(owner * cols, cols), cols), :]

    def wo_copy(k, owner, device):
        return pltpu.make_async_remote_copy(
            src_ref=wo_part(owner), dst_ref=wo_rows(head), send_sem=wsend.at[k], recv_sem=wrecv.at[k],
            device_id=device, device_id_type=MESH)

    wo_copies = [
        wo_copy(0, mate, (tm, mate)),
        wo_copy(1, far, (tm, far)),
        wo_copy(2, far_mate, (pair, far_mate)),
    ]

    for p in range(2):
        own_far(p).start()
        own_pair(p).start()
    for load in loads:
        load.start()
    mate_own().start()
    for load in loads:
        load.wait()
    arrived(band(0, 0, rows, mate), 4, 0)

    def store_kv(slab, m, key_sums, value_sums):
        b, r = 2 * slab + m // 2, pl.ds(pl.multiple_of((m % 2) * step_rows, step_rows), step_rows)
        for h in range(heads):
            c = slice(h * HEAD_DIM, (h + 1) * HEAD_DIM)
            kv[b, r, c] = normed(key_sums[:, c], k_gain[...]).astype(jnp.bfloat16)
        kv[b, r, cols:] = value_sums.astype(jnp.bfloat16)

    def step(p, carry):
        @pl.when(p < STEPS)
        def _():
            arrived(band(0, at(p), step_rows, far), 0, p)
            relay_far(p).start()
            mate_far(p).start()
            arrived(band(1, at(p), step_rows, far), 1, p)
            relay_pair(p).start()
            mate_pair(p).start()

        @pl.when(p < STEPS - 2)
        def _():
            own_far(p + 2).start()
            own_pair(p + 2).start()

        @pl.when(p == STEPS)
        def _():
            for c in wo_copies:
                c.start()

        @pl.when(p >= 1)
        def _():
            m = p - 1
            arrived(band(1, at(m), half, head), 2, m)
            arrived(band(1, at(m) + half, half, head), 3, m)
            mate_relayed(m).start()
            arrived(band(0, at(m), step_rows, far_mate), 5, m)
            arrived(band(1, at(m), step_rows, far_mate), 6, m)
            arrived(band(1, at(m), step_rows, mate), 7, m)
            sums = jnp.dot(x[1, pl.ds(at(m), step_rows), :], w[:, cols:], preferred_element_type=jnp.float32)
            store_kv(1, m, sums[:, :cols], sums[:, cols:])
            z_copy(m).start()
            sums = jnp.dot(x[0, pl.ds(at(m), step_rows), :], w[...], preferred_element_type=jnp.float32)
            for h in range(heads):
                c = slice(h * HEAD_DIM, (h + 1) * HEAD_DIM)
                q[pl.ds(at(m), step_rows), c] = normed(sums[:, c], q_gain[...]).astype(jnp.bfloat16)
            store_kv(0, m, sums[:, cols:2 * cols], sums[:, 2 * cols:])

        return carry

    lax.fori_loop(0, STEPS + 1, step, 0)

    def drain(p, carry):
        for c in (own_far(p), own_pair(p), relay_far(p), relay_pair(p), mate_far(p), mate_pair(p), mate_relayed(p)):
            c.wait_send()
        arrived(kv_rows(2, p), 8, p)
        z_copy(p).wait_send()
        return carry

    lax.fori_loop(0, STEPS, drain, 0)
    mate_own().wait_send()

    scaling = 1.0 / math.sqrt(HEAD_DIM)
    base = 2 * tm
    first = slot[base] - base

    def attend(b, carry):
        t = jnp.clip(first + b - 2 * first * b, 0, 1)
        places = []
        for j in range(nbr.shape[1]):
            block = slot[jnp.clip(nbr[t, j], 0, slot.shape[0] - 1)] - base
            block = jnp.where(block < 0, block + 6 - 2 * y_hi, jnp.where(block >= 2, block + 2 * y_hi, block))
            places.append(jnp.clip(block, 0, kv.shape[0] - 1))
        r = pl.ds(pl.multiple_of(b * tile, tile), tile)
        for h in range(heads):
            c = slice(h * HEAD_DIM, (h + 1) * HEAD_DIM)
            cv = slice(cols + h * HEAD_DIM, cols + (h + 1) * HEAD_DIM)
            qh = q[r, c]
            total, out = None, None
            for place in places:
                scores = lax.dot_general(
                    qh, kv[place, :, c], (((1,), (1,)), ((), ())), preferred_element_type=jnp.float32)
                raised = jnp.exp(scores * scaling)
                part = jnp.sum(raised, axis=-1, keepdims=True)
                got = jnp.dot(raised.astype(jnp.bfloat16), kv[place, :, cv], preferred_element_type=jnp.float32)
                total = part if total is None else total + part
                out = got if out is None else out + got
            o_ref[r, c] = (out / total).astype(jnp.bfloat16)
        return carry

    lax.fori_loop(0, 2, attend, 0)

    for k, owner in enumerate((mate, far, far_mate)):
        wo_copies[k].wait_send()
        pltpu.make_async_remote_copy(
            src_ref=wo_rows(owner), dst_ref=wo_rows(owner), send_sem=wsend.at[k], recv_sem=wrecv.at[k],
            device_id=(tm, mate), device_id_type=MESH).wait_recv()


def z_moved(tm, by):
    return tm // SAME_X * SAME_X + (tm // 2 % N_Z + by + N_Z) % N_Z * 2 + tm % 2


def way_round(distance):
    if distance in (2, N_Z - 2):
        return 2, -3 if distance == 2 else 3
    if distance in (3, N_Z - 3):
        return 3, -2 if distance == 3 else 2
    return 0, 0


def hand_kernel(r, o, g, relayed, recv, sent, joined, passed):
    tm, head = lax.axis_index("tm"), lax.axis_index("head")
    n_tm = lax.axis_size("tm")
    rows, cols = o.shape
    chunk_rows = rows // CHUNKS
    mate, far, far_mate = core_mate(head), across(head), across(core_mate(head))
    to, source = (tm + r) % n_tm, (tm - r + n_tm) % n_tm
    (n_low, by_low), (n_high, by_high) = way_round(r // 2 % N_Z), way_round((r + 1) // 2 % N_Z)
    relays = n_low + n_high > 0

    def either(low, high, device):
        return low if low == high else low + (high - low) * (device % 2)

    n_mine, n_source = either(n_low, n_high, tm), either(n_low, n_high, source)
    relay = z_moved(tm, either(by_low, by_high, tm))
    relay_for = z_moved(tm, -either(by_low, by_high, tm))
    relay_to = (relay_for + r) % n_tm
    source_relay = z_moved(source, either(by_low, by_high, source))

    def when(count, act):
        if isinstance(count, int):
            if count:
                act()
        else:
            pl.when(count > 0)(act)

    def band(start, count, owner):
        return g.at[pl.ds(start, count), pl.ds(pl.multiple_of(owner * cols, cols), cols)]

    def at(p):
        return pl.multiple_of(p * chunk_rows, chunk_rows)

    def own(p):
        return o.at[pl.ds(at(p), chunk_rows), :]

    barrier = pltpu.get_barrier_semaphore()

    def greet(device):
        pl.semaphore_signal(barrier, inc=1, device_id=device, device_id_type=MESH)

    for device in ((tm, mate), (tm, far), (source, head)):
        greet(device)
    if relays:
        when(n_mine, lambda: greet((relay_for, head)))
        when(n_source, lambda: greet((source_relay, head)))
    pl.semaphore_wait(barrier, either(5 if n_low else 3, 5 if n_high else 3, tm))

    def copy(src, dst, device, arrival, departure=None):
        return pltpu.make_async_remote_copy(
            src_ref=src, dst_ref=dst, send_sem=sent if departure is None else departure, recv_sem=arrival,
            device_id=device, device_id_type=MESH)

    def hand(p):
        return copy(own(p), band(at(p), chunk_rows, head), (to, head), recv.at[0, p])

    def to_relay(p):
        return copy(own(p), relayed.at[p], (relay, head), recv.at[2, p])

    def from_relay(p):
        return copy(relayed.at[p], band(at(p), chunk_rows, head), (relay_to, head), recv.at[0, p], passed.at[p])

    def pass_on(p, owner, device, arrival):
        block = band(at(p), chunk_rows, owner)
        return copy(block, block, device, arrival)

    def loop(low, high, act):
        def body(p, carry):
            act(p)
            return carry
        lax.fori_loop(low, high, body, 0)

    if relays:
        loop(0, n_mine, lambda p: to_relay(p).start())
    loop(n_mine, CHUNKS, lambda p: hand(p).start())

    def relay_one(p):
        to_relay(p).wait_recv()
        from_relay(p).start()

    if relays:
        loop(0, n_mine, relay_one)

    def spread(k):
        p = k
        if relays:
            turned = jnp.logical_and(k % 2 == 1, k // 2 < n_source)
            p = jnp.where(turned, k // 2, n_source + k - jnp.minimum((k + 1) // 2, n_source))
        pass_on(p, head, (tm, mate), recv.at[0, p]).wait_recv()
        pass_on(p, head, (tm, far), recv.at[1, p]).start()
        pass_on(p, head, (tm, mate), joined).start()

    def second(k):
        p = k
        if relays:
            turned = jnp.logical_and(k % 2 == 1, k // 2 < n_source)
            p = jnp.where(turned, k // 2, n_source + k - jnp.minimum((k + 1) // 2, n_source))
        pass_on(p, far, (tm, mate), recv.at[1, p]).wait_recv()
        pass_on(p, far, (tm, mate), joined).start()

    loop(0, CHUNKS, spread)
    loop(0, CHUNKS, second)
    two = g.at[:, pl.ds(0, 2 * cols)]
    copy(two, two, (tm, mate), joined).wait_recv()
    copy(g, g, (tm, mate), joined).wait_send()
    if relays:
        loop(0, n_mine, lambda p: from_relay(p).wait_send())


def handed_over(r, o):
    rows, cols = o.shape
    return pl.pallas_call(
        functools.partial(hand_kernel, r),
        name="hand",
        out_shape=jax.ShapeDtypeStruct((rows, 4 * cols), jnp.bfloat16),
        in_specs=[pl.BlockSpec(memory_space=pl.ANY)],
        out_specs=pl.BlockSpec(memory_space=pl.ANY),
        scratch_shapes=[
            pltpu.VMEM((3, rows // CHUNKS, cols), jnp.bfloat16),
            pltpu.SemaphoreType.DMA((3, CHUNKS)),
            pltpu.SemaphoreType.DMA,
            pltpu.SemaphoreType.DMA,
            pltpu.SemaphoreType.DMA((3,)),
        ],
        compiler_params=pltpu.CompilerParams(
            collective_id=2 + r, has_side_effects=True, vmem_limit_bytes=HAND_LIMIT
        ),
    )(o)


def product_kernel(g, wo, out):
    out[...] = jnp.dot(g[...], wo[...], preferred_element_type=jnp.float32).astype(jnp.bfloat16)


def per_device(
    latents, w_query, w_key, w_value, q_gain, k_gain, w_out, neighbours, tile_slot, slab_dest
):
    rows, width = latents.shape
    cols = w_query.shape[1]
    any_spec = pl.BlockSpec(memory_space=pl.ANY)
    vmem_spec = pl.BlockSpec(memory_space=pltpu.VMEM)
    smem_spec = pl.BlockSpec(memory_space=pltpu.SMEM)
    bf16 = jnp.bfloat16
    attention, wo = pl.pallas_call(
        attend_kernel,
        name="attend",
        out_shape=(
            jax.ShapeDtypeStruct((rows, cols), bf16),
            jax.ShapeDtypeStruct((4 * cols, width), bf16),
        ),
        in_specs=[any_spec] * 4 + [vmem_spec] * 2 + [any_spec] + [smem_spec] * 2,
        out_specs=(vmem_spec, vmem_spec),
        scratch_shapes=[
            pltpu.VMEM((2, rows, 4 * width), bf16),
            pltpu.VMEM((4 * width, 3 * cols), bf16),
            pltpu.VMEM((6, rows // 2, 2 * cols), bf16),
            pltpu.VMEM((rows, cols), bf16),
            pltpu.SemaphoreType.DMA((9, STEPS)),
            pltpu.SemaphoreType.DMA((9, STEPS)),
            pltpu.SemaphoreType.DMA((3,)),
            pltpu.SemaphoreType.DMA((3,)),
            pltpu.SemaphoreType.DMA((5,)),
        ],
        compiler_params=pltpu.CompilerParams(
            collective_id=1, has_side_effects=True, vmem_limit_bytes=VMEM_LIMIT
        ),
    )(
        latents, w_query, w_key, w_value, q_gain.reshape(1, -1), k_gain.reshape(1, -1), w_out, neighbours, tile_slot
    )
    n_tm = lax.axis_size("tm")
    hands = [functools.partial(handed_over, r) for r in range(1, n_tm)]
    gathered = lax.switch(slab_dest[0] - 1, hands, attention)
    return pl.pallas_call(
        product_kernel,
        name="product",
        out_shape=jax.ShapeDtypeStruct((rows, width), bf16),
        grid=(3,),
        in_specs=[
            pl.BlockSpec((rows // 3, 4 * cols), lambda i: (i, 0)),
            pl.BlockSpec((4 * cols, width), lambda i: (0, 0)),
        ],
        out_specs=pl.BlockSpec((rows // 3, width), lambda i: (i, 0)),
        compiler_params=pltpu.CompilerParams(vmem_limit_bytes=PRODUCT_LIMIT),
    )(gathered, wo)


def solution(mesh):
    return jax.shard_map(
        per_device,
        mesh=mesh,
        in_specs=(
            P("tm", "head"),
            P(None, "head"),
            P(None, "head"),
            P(None, "head"),
            P(),
            P(),
            P("head", None),
            P("tm", None),
            P(),
            P(),
        ),
        out_specs=P("tm", "head"),
        check_vma=False,
    )
```
